32 devices in a mesh: gx: 4 (over z), gy: 8 (over y, x, core).
Axes of the slice: x: 2, y: 2, z: 4, core: 2. Of those that a mesh axis runs over, the one named last changes fastest.
Arguments:
- objective_grad: bfloat16 [64, 2048, 128], P('gx', 'gy'), may hold values from -6 to 6
- adjoint_start: bfloat16 [64, 2048, 128], P('gx', 'gy'), may hold values from -6 to 6
- levels: int32 [64, 2048], P('gx', 'gy'), may hold values from 1 to 16
- stiffness: bfloat16 [9, 64, 64], replicated
- row_cells: int32 [131072], P(('gx', 'gy')), may hold values from 0 to 4095
- row_front: int32 [131072, 1], P(('gx', 'gy')), may hold values from 0 to 63; in each aligned block of 4096 rows (0 to 4095, 4096 to 8191, ...) at most 128 rows name the same one
- row_pos: int32 [131072], P(('gx', 'gy')), may hold values from 0 to 511
- front_place: int32 [64], replicated, may hold values from 0 to 63, each once
- schur: bfloat16 [64, 512, 512], P(('gx', 'gy')), may hold values from -0.25 to 0.25
Outputs:
- adjoint: float32 [64, 2048, 128], P('gx', 'gy')
- front_values: float32 [64, 512, 128], P(('gx', 'gy'))
The draws below stay inside these ranges and needn't reach their ends.
Inputs may be any that keep to these rules, and one draw needn't show every extreme that they name: `row_cells`: a segment of the listing subdomain's 16 x 256 block, counted row-major. `row_front`: among the rows of one subdomain at most 128 name the same front, a bound that some block reaches of them. `front_place`: each place is taken once; place q is held by device q // 2 in the order gx 8 + gy.
All inputs are finite; a program needn't handle non-finite values.
Results may differ from the reference program's by a relative error of at most 0.0042.
Values may be sent and summed in bfloat16 or wider, within the bound.
A program may use at most 128 MiB of HBM per device.

```python
import math
import jax
import jax.numpy as jnp
import numpy as np
from jax import lax

CX = 16
CY = 256
DOF = 64
LEVELS = 16
ROWS_DEV = 4096
FSIZE = 512
NX = 64
NY = 2048
ROW = 128
FRONTS = 64
ROWS = 131072
CAP = 128
N_GX = 4
N_GY = 8


def draw_stiffness(key, part):
    noise = jax.random.normal(key, (9, DOF, DOF), jnp.float32)
    center = (jnp.arange(9) == 4).astype(jnp.float32)[:, None, None]
    scales = 0.08 - 0.03 * center
    return (center * jnp.eye(DOF, dtype=jnp.float32)[None, :, :] + scales * noise).astype(jnp.bfloat16)


def set_ends(values, key, smallest, high):
    index_at = [jax.random.randint(jax.random.fold_in(key, axis), (), 0, length) for axis, length in enumerate(values.shape)]
    widest = values.shape.index(max(values.shape))
    next_to = index_at[:widest] + [(index_at[widest] + 1) % values.shape[widest]] + index_at[widest + 1:]
    return values.at[tuple(index_at)].set(smallest).at[tuple(next_to)].set(high)


def shard_levels(rng, shape, split, least, high):
    loudness = 1.0
    for dim, parts in split:
        draws = jax.random.uniform(jax.random.fold_in(jax.random.fold_in(rng, 6), dim), (parts,), jnp.float32, least / len(split), high / len(split))
        loudness = loudness * jnp.repeat(jnp.exp(draws), shape[dim] // parts).reshape((-1,) + (1,) * (len(shape) - 1 - dim))
    return loudness


def assign_block(key, own, number, rows, number_of, top, most, skew):
    sequence = jax.random.permutation(key, number_of)
    heavy_load, ordinary = shares(number_of, rows * top, most, skew, True), shares(number_of, rows * top, most, skew, False)
    places = jnp.arange(number_of)

    def named(sizes, turn):
        used = int((sizes > 0).sum())
        fixed = max(1, used // 4)
        passed = fixed + (places - fixed + turn * (used - fixed)) % max(1, number_of - fixed)
        return jnp.zeros((number_of,), jnp.int32).at[sequence[jnp.where(places < fixed, places, passed)]].set(jnp.asarray(sizes, jnp.int32))

    sizes = jnp.where(number % 4 == 0, named(heavy_load, number // 4), named(ordinary, number - number // 4 - 1))
    mixed = jax.random.permutation(jax.random.fold_in(own, 3), number_of)
    source_of, taker = mixed[0:number_of // 2 * 2:2], mixed[1:number_of // 2 * 2:2]
    margin = jnp.minimum(sizes[source_of] - 1, most - sizes[taker]) // 2
    margin = jnp.where((source_of == sequence[0]) | (taker == sequence[0]) | (sizes[taker] == 0), 0, jnp.maximum(margin, 0))
    passed = jax.random.randint(jax.random.fold_in(own, 4), (number_of // 2,), 0, 1 << 20) % (margin + 1)
    sizes = sizes.at[source_of].add(-passed).at[taker].add(passed)
    labels = jnp.searchsorted(jnp.cumsum(sizes), jnp.arange(rows * top), side="right").astype(jnp.int32)
    table = labels.reshape(top, rows).T
    table = table[jax.random.permutation(jax.random.fold_in(own, 1), rows)]
    turn = jax.random.randint(jax.random.fold_in(own, 2), (rows, 1), 0, top)
    return jnp.take_along_axis(table, (jnp.arange(top)[None, :] + turn) % top, axis=1)


def shares(amount, total, limit, slope, full):
    portions = [(1 << 20) // math.isqrt(grade ** slope) + 1 for grade in range(1, amount + 1)]
    largest = limit if full else min(limit, max(-(-total // amount), total * portions[0] // sum(portions)))
    least = 1 if total - largest >= amount - 1 else 0
    given, rest = [largest] + [least] * (amount - 1), total - largest - least * (amount - 1)
    while rest > 0:
        candidates = [i for i in range(1, amount) if given[i] < largest] or [i for i in range(1, amount) if given[i] < limit]
        whole, remaining = sum([portions[i] for i in candidates]), rest
        for i in candidates:
            addition = min(limit - given[i], max(1, remaining * portions[i] // whole), rest)
            given[i] = given[i] + addition
            rest = rest - addition
    return np.array(given)


def gaussian(stream_key, extent, spread, most, split=(), kind=jnp.bfloat16):
    entries = jax.random.normal(stream_key, extent, jnp.float32) * spread
    if len(split) > 0:
        entries = shard_levels(stream_key, extent, split, -0.22, 0.18) * entries
    return jnp.clip(entries, min=-most, max=most).astype(kind)


def setup_inputs(seed: int = 0) -> dict:
    keys = jax.random.split(jax.random.key(seed), 10)
    objective_grad = gaussian(keys[0], (NX, NY, ROW), 1.0, 6.0, ((0, 4), (1, 8)))
    adjoint_start = gaussian(keys[1], (NX, NY, ROW), 1.0, 6.0, ((0, 4), (1, 8)))
    levels = set_ends(jax.random.randint(keys[2], (NX, NY), 1, LEVELS + 1), jax.random.fold_in(keys[2], 1), 1, LEVELS).astype(jnp.int32)
    stiffness = draw_stiffness(jax.random.fold_in(keys[9], 71), 0)
    row_cells = set_ends(jax.random.randint(keys[4], (ROWS,), 0, CX * CY), jax.random.fold_in(keys[4], 1), 0, (CX * CY) - 1).astype(jnp.int32)
    row_front_keys = jax.random.split(jax.random.fold_in(keys[5], 1), ROWS // ROWS_DEV)
    row_front_turns = jax.random.permutation(jax.random.fold_in(keys[5], 3), ROWS // ROWS_DEV)
    row_front = jax.vmap(lambda own, number: assign_block(jax.random.fold_in(keys[5], 2), own, number, ROWS_DEV, FRONTS, 1, CAP, 2))(row_front_keys, row_front_turns).reshape((ROWS, 1))
    row_pos = set_ends(jax.random.randint(keys[6], (ROWS,), 0, FSIZE), jax.random.fold_in(keys[6], 1), 0, FSIZE - 1).astype(jnp.int32)
    front_place = jax.random.permutation(keys[7], FRONTS).astype(jnp.int32)
    schur = gaussian(keys[8], (FRONTS, FSIZE, FSIZE), FSIZE ** -0.5, 0.25, ((0, 32),))
    return {"objective_grad": objective_grad, "adjoint_start": adjoint_start, "levels": levels, "stiffness": stiffness, "row_cells": row_cells, "row_front": row_front, "row_pos": row_pos, "front_place": front_place, "schur": schur}


soft_floor = 0.001
relax_rate = 0.5


def cell_weight(levels):
    ratio = levels.astype(jnp.float32) / LEVELS
    return soft_floor + (1.0 - soft_floor) * ratio * ratio * ratio


def stiffness_apply(padded, stiffness, out_rows, out_cols):
    summed = jnp.zeros((out_rows, out_cols, padded.shape[2]), jnp.float32)
    for shift_row in (-1, 0, 1):
        for shift_col in (-1, 0, 1):
            source = padded[1 - shift_row:1 - shift_row + out_rows, 1 - shift_col:1 - shift_col + out_cols, :]
            flattened = source.reshape(-1, stiffness.shape[1])
            product = jnp.dot(flattened, stiffness[3 * (shift_row + 1) + (shift_col + 1)], preferred_element_type=jnp.float32)
            summed = summed + product.reshape(out_rows, out_cols, -1)
    return summed


def reference(objective_grad, adjoint_start, levels, stiffness, row_cells, row_front, row_pos, front_place, schur):
    weight = cell_weight(levels)
    grad_full = objective_grad.astype(jnp.float32)
    adjoint_now = adjoint_start.astype(jnp.float32)
    for sweep in range(3):
        scaled = (weight[:, :, None] * adjoint_now).astype(jnp.bfloat16)
        padded = jnp.pad(scaled, ((1, 1), (1, 1), (0, 0)))

        def one_block(index):
            start = (index * CX).astype(jnp.int32)
            source = lax.dynamic_slice_in_dim(padded, start, CX + 2, 0)
            return stiffness_apply(source, stiffness, CX, NY)

        image = lax.map(one_block, jnp.arange(N_GX, dtype=jnp.int32)).reshape(NX, NY, ROW)
        adjoint_now = adjoint_now + relax_rate * (grad_full - image)
    sent_field = adjoint_now.astype(jnp.bfloat16)
    owner_dev = jnp.arange(ROWS, dtype=jnp.int32) // ROWS_DEV
    owner_gx = owner_dev // N_GY
    owner_gy = owner_dev % N_GY
    cell_x = owner_gx * CX + row_cells // CY
    cell_y = owner_gy * CY + row_cells % CY
    sent_rows = sent_field[cell_x, cell_y]
    places = front_place[row_front[:, 0]]
    assembled = jnp.zeros((FRONTS, FSIZE, ROW), jnp.float32).at[places, row_pos].add(sent_rows.astype(jnp.float32))
    assembled = assembled.astype(jnp.bfloat16)
    front_values = jnp.einsum("qab,qbl->qal", schur.astype(jnp.float32), assembled.astype(jnp.float32))
    return adjoint_now, front_values
```

```python
import functools

import jax
import jax.numpy as jnp
from jax import lax
from jax.experimental import pallas as pl
from jax.experimental.pallas import tpu as pltpu
from jax.sharding import PartitionSpec as P

LEVELS = 16

soft_floor = 0.001
relax_rate = 0.5

MESH = pl.DeviceIdType.MESH
PASSES = 3
SIDES = ((-1, 0), (1, 0), (0, -1), (0, 1), (-1, -1), (-1, 1), (1, -1), (1, 1))


def cell_weight(levels):
    ratio = levels.astype(jnp.float32) / LEVELS
    return soft_floor + (1.0 - soft_floor) * ratio * ratio * ratio


def relax_kernel(
    size_x,
    size_y,
    grad_ref,
    start_ref,
    weight_ref,
    blocks_ref,
    lam_ref,
    wide_ref,
    shifted_ref,
    line_ref,
    big_ref,
    edge_ref,
    edge_send_ref,
    row_in_ref,
    col_in_ref,
    send_sem,
    recv_sem,
):
    rows, cols, width = grad_ref.shape
    gx, gy = lax.axis_index("gx"), lax.axis_index("gy")

    def exists(side):
        dx, dy = side
        held = None
        for here, step, size in ((gx, dx, size_x), (gy, dy, size_y)):
            if step:
                inside = (here + step >= 0) & (here + step < size)
                held = inside if held is None else held & inside
        return held

    def place(side):
        return (gx + side[0], gy + side[1])

    row_in_ref[...] = jnp.zeros_like(row_in_ref)
    col_in_ref[...] = jnp.zeros_like(col_in_ref)

    barrier = pltpu.get_barrier_semaphore()
    for side in SIDES:

        @pl.when(exists(side))
        def _(side=side):
            pl.semaphore_signal(barrier, inc=1, device_id=place(side), device_id_type=MESH)

    for b in range(3):
        shifted_ref[b, 0] = jnp.zeros((cols, width), jnp.bfloat16)
        shifted_ref[b, rows + 1] = jnp.zeros((cols, width), jnp.bfloat16)
    line_ref[0:8, :] = jnp.zeros((8, width), jnp.float32)
    line_ref[8 + cols : 16 + cols, :] = jnp.zeros((8, width), jnp.float32)

    for i in range(4):
        for b in range(3):
            for j in range(2):
                a = j + 1 - i
                at = (pl.ds((3 * i + b) * width, width), pl.ds(j * width, width))
                if -1 <= a <= 1:
                    big_ref[at] = blocks_ref[3 * (a + 1) + b]
                else:
                    big_ref[at] = jnp.zeros((width, width), jnp.bfloat16)

    for r in range(rows):
        wide_ref[r] = jnp.broadcast_to(weight_ref[:, r : r + 1], (cols, width))

    def take_start(r, carry):
        lam_ref[r] = start_ref[r].astype(jnp.float32)
        return carry

    lax.fori_loop(0, rows, take_start, 0)

    near_x = 1 + jnp.minimum(gx, 1) + jnp.minimum(size_x - 1 - gx, 1)
    near_y = 1 + jnp.minimum(gy, 1) + jnp.minimum(size_y - 1 - gy, 1)
    pl.semaphore_wait(barrier, near_x * near_y - 1)

    def copies(step):
        made = []
        for n, side in enumerate(SIDES):
            if side[1] == 0:
                source = shifted_ref.at[1, 1 if side[0] < 0 else rows]
                target = row_in_ref.at[step, 1 if side[0] < 0 else 0]
            else:
                source = edge_send_ref.at[0 if side[1] < 0 else 1]
                target = col_in_ref.at[step, SIDES.index((-side[0], -side[1])) - 2]
            made.append(
                pltpu.make_async_remote_copy(
                    src_ref=source,
                    dst_ref=target,
                    send_sem=send_sem.at[step, n],
                    recv_sem=recv_sem.at[step, SIDES.index((-side[0], -side[1]))],
                    device_id=place(side),
                    device_id_type=MESH,
                )
            )
        return made

    def arrivals(step):
        made = []
        for n, side in enumerate(SIDES):
            if side[1] == 0:
                target = row_in_ref.at[step, 0 if side[0] < 0 else 1]
            else:
                target = col_in_ref.at[step, n - 2]
            made.append((side, target, recv_sem.at[step, n]))
        return made

    def spread():
        return [line_ref[9 - b : 9 - b + cols, :].astype(jnp.bfloat16) for b in range(3)]

    for step in range(PASSES):

        def produce(r, carry):
            scaled = wide_ref[r] * lam_ref[r]
            line_ref[8 : 8 + cols, :] = scaled
            left, middle, right = spread()
            shifted_ref[0, r + 1] = left
            shifted_ref[1, r + 1] = middle
            shifted_ref[2, r + 1] = right
            edge_ref[0, pl.ds(r, 1), :] = scaled[0:1, :]
            edge_ref[1, pl.ds(r, 1), :] = scaled[cols - 1 : cols, :]
            return carry

        lax.fori_loop(0, rows, produce, 0)
        edge_send_ref[...] = edge_ref[:, 0:rows, :].astype(jnp.bfloat16)

        sends = copies(step)
        for side, copy in zip(SIDES, sends):

            @pl.when(exists(side))
            def _(copy=copy):
                copy.start()

        def interior(t, carry):
            r = 4 * t
            lhs = jnp.concatenate(
                [
                    jnp.concatenate(
                        [shifted_ref[b, r + 2 * p + i] for i in range(4) for b in range(3)], axis=1
                    )
                    for p in range(2)
                ],
                axis=0,
            )
            image = jnp.dot(lhs, big_ref[...], preferred_element_type=jnp.float32)
            for p in range(2):
                for j in range(2):
                    at = r + 2 * p + j
                    part = image[p * cols : (p + 1) * cols, j * width : (j + 1) * width]
                    lam_ref[at] = lam_ref[at] + relax_rate * (
                        grad_ref[at].astype(jnp.float32) - part
                    )
            return carry

        lax.fori_loop(0, rows // 4, interior, 0)

        for n, (side, copy) in enumerate(zip(SIDES, sends)):

            @pl.when(exists(side))
            def _(copy=copy):
                copy.wait_send()

        for side, copy in zip(SIDES, sends):

            @pl.when(exists(side))
            def _(side=side, step=step):
                target, semaphore = [x[1:] for x in arrivals(step) if x[0] == side][0]
                pltpu.make_async_remote_copy(
                    src_ref=target,
                    dst_ref=target,
                    send_sem=send_sem.at[step, 0],
                    recv_sem=semaphore,
                    device_id=place(side),
                    device_id_type=MESH,
                ).wait_recv()

        for end in range(2):
            line_ref[8 : 8 + cols, :] = row_in_ref[step, end].astype(jnp.float32)
            lhs = jnp.concatenate(spread(), axis=1)
            depth = 3 * width
            piece = (
                big_ref[0:depth, 0:width]
                if end == 0
                else big_ref[3 * depth : 4 * depth, width : 2 * width]
            )
            more = jnp.dot(lhs, piece, preferred_element_type=jnp.float32)
            at = 0 if end == 0 else rows - 1
            lam_ref[at] = lam_ref[at] - relax_rate * more

        for end in range(2):
            edge_ref[end, 8 : 8 + rows, :] = col_in_ref[step, end].astype(jnp.float32)
            upper = col_in_ref[step, 2 + end].astype(jnp.float32)
            lower = col_in_ref[step, 4 + end].astype(jnp.float32)
            edge_ref[end, 7:8, :] = upper[rows - 1 : rows, :]
            edge_ref[end, 8 + rows : 9 + rows, :] = lower[0:1, :]
            b = 2 if end == 0 else 0
            more = jnp.zeros((rows, width), jnp.float32)
            for a in (-1, 0, 1):
                source = edge_ref[end, 8 - a : 8 - a + rows, :].astype(jnp.bfloat16)
                more = more + jnp.dot(
                    source, blocks_ref[3 * (a + 1) + b], preferred_element_type=jnp.float32
                )
            at = 0 if end == 0 else cols - 1
            for r in range(rows):
                lam_ref[r, at : at + 1, :] = (
                    lam_ref[r, at : at + 1, :] - relax_rate * more[r : r + 1, :]
                )


def relax(grad, start, weight, blocks, size_x, size_y):
    rows, cols, width = grad.shape
    vmem = pl.BlockSpec(memory_space=pltpu.VMEM)
    return pl.pallas_call(
        functools.partial(relax_kernel, size_x, size_y),
        out_shape=jax.ShapeDtypeStruct((rows, cols, width), jnp.float32),
        in_specs=[vmem] * 4,
        out_specs=vmem,
        scratch_shapes=[
            pltpu.VMEM((rows, cols, width), jnp.float32),
            pltpu.VMEM((3, rows + 2, cols, width), jnp.bfloat16),
            pltpu.VMEM((cols + 16, width), jnp.float32),
            pltpu.VMEM((12 * width, 2 * width), jnp.bfloat16),
            pltpu.VMEM((2, rows + 16, width), jnp.float32),
            pltpu.VMEM((2, rows, width), jnp.bfloat16),
            pltpu.VMEM((PASSES, 2, cols, width), jnp.bfloat16),
            pltpu.VMEM((PASSES, 6, rows, width), jnp.bfloat16),
            pltpu.SemaphoreType.DMA((PASSES, 8)),
            pltpu.SemaphoreType.DMA((PASSES, 8)),
        ],
        compiler_params=pltpu.CompilerParams(
            collective_id=0, has_side_effects=True, vmem_limit_bytes=48 * 1024 * 1024
        ),
        cost_estimate=pl.CostEstimate(
            flops=6 * 2 * rows * cols * width * 9 * width,
            bytes_accessed=8 * rows * cols * width,
            transcendentals=0,
        ),
    )(grad, start, weight, blocks)


def table_kernel(front_ref, cell_ref, pos_ref, place_ref, cells_ref, spots_ref, sums_ref):
    count, capacity = cells_ref.shape
    total = front_ref.shape[1]
    block = 256
    order = lax.broadcasted_iota(jnp.int32, (count, count), 0)
    moved = (order == place_ref[...]).astype(jnp.float32).astype(jnp.bfloat16)
    before = (
        lax.broadcasted_iota(jnp.int32, (block, block), 0)
        < lax.broadcasted_iota(jnp.int32, (block, block), 1)
    )
    before = before.astype(jnp.float32).astype(jnp.bfloat16)
    carry = jnp.zeros((count, 1), jnp.float32)
    sums_ref[...] = jnp.zeros_like(sums_ref)
    for n in range(total // block):
        at = slice(n * block, (n + 1) * block)
        named = lax.broadcasted_iota(jnp.int32, (count, block), 0) == front_ref[:, at]
        named = named.astype(jnp.float32).astype(jnp.bfloat16)
        member = jnp.dot(moved, named, preferred_element_type=jnp.float32)
        inside = jnp.dot(
            member.astype(jnp.bfloat16), before, preferred_element_type=jnp.float32
        )
        rank = jnp.sum(member * (inside + carry), axis=0, keepdims=True)
        carry = carry + jnp.sum(member, axis=1, keepdims=True)
        slot = lax.broadcasted_iota(jnp.int32, (capacity, block), 0) == rank.astype(jnp.int32)
        slot = slot.astype(jnp.float32).astype(jnp.bfloat16)
        cell, pos = cell_ref[:, at], pos_ref[:, at]
        pieces = (cell // 64, cell % 64, pos // 16, pos % 16 + 1)
        lhs = jnp.concatenate([member * p.astype(jnp.float32) for p in pieces], axis=0)
        sums_ref[...] += lax.dot_general(
            lhs.astype(jnp.bfloat16),
            slot,
            (((1,), (1,)), ((), ())),
            preferred_element_type=jnp.float32,
        )
    part = [sums_ref[n * count : (n + 1) * count, :].astype(jnp.int32) for n in range(4)]
    cells_ref[...] = part[0] * 64 + part[1]
    spots_ref[...] = part[2] * 16 + part[3] - 1


def row_table(row_front, row_cells, row_pos, front_place, capacity):
    count = front_place.shape[0]
    shape = jax.ShapeDtypeStruct((count, capacity), jnp.int32)
    return pl.pallas_call(
        table_kernel,
        out_shape=(shape, shape),
        in_specs=[pl.BlockSpec(memory_space=pltpu.VMEM)] * 4,
        out_specs=(pl.BlockSpec(memory_space=pltpu.VMEM),) * 2,
        scratch_shapes=[pltpu.VMEM((4 * count, capacity), jnp.float32)],
        compiler_params=pltpu.CompilerParams(vmem_limit_bytes=32 * 1024 * 1024),
    )(
        row_front.reshape(1, -1),
        row_cells.reshape(1, -1),
        row_pos.reshape(1, -1),
        front_place.reshape(1, -1),
    )


def pick_kernel(cells_ref, field_ref, out_ref, held_ref):
    total = out_ref.shape[0]
    step = 32

    def some(t, carry):
        for u in range(step):
            at = t * step + u
            held_ref[pl.ds(at, 1), :] = field_ref[pl.ds(cells_ref[at], 1), :]
        return carry

    lax.fori_loop(0, total // step, some, 0)
    out_ref[...] = held_ref[...].astype(out_ref.dtype)


def pick(cells, field):
    total, width = cells.shape[0], field.shape[1]
    vmem = pl.BlockSpec(memory_space=pltpu.VMEM)
    return pl.pallas_call(
        pick_kernel,
        out_shape=jax.ShapeDtypeStruct((total, width), jnp.bfloat16),
        in_specs=[pl.BlockSpec(memory_space=pltpu.SMEM), vmem],
        out_specs=vmem,
        scratch_shapes=[pltpu.VMEM((total, width), jnp.float32)],
        compiler_params=pltpu.CompilerParams(vmem_limit_bytes=32 * 1024 * 1024),
    )(cells, field)


def local(
    size_x,
    size_y,
    objective_grad,
    adjoint_start,
    levels,
    stiffness,
    row_cells,
    row_front,
    row_pos,
    front_place,
    schur,
):
    rows, cols, width = objective_grad.shape
    freedom = stiffness.shape[1]
    cases = width // freedom
    same = jnp.eye(cases, dtype=stiffness.dtype)
    blocks = (same[None, :, None, :, None] * stiffness[:, None, :, None, :]).reshape(
        9, width, width
    )
    adjoint = relax(
        objective_grad, adjoint_start, cell_weight(levels).T, blocks, size_x, size_y
    )

    front_count = front_place.shape[0]
    devices = size_x * size_y
    owned, front_size = schur.shape[0], schur.shape[1]
    capacity = 2 * row_cells.shape[0] // front_count
    cells, spots = row_table(row_front, row_cells, row_pos, front_place, capacity)
    rows_out = pick(cells.reshape(-1), adjoint.reshape(rows * cols, width))
    slot_total = owned * capacity
    spread = functools.partial(
        lax.all_to_all, axis_name=("gx", "gy"), split_axis=0, concat_axis=0, tiled=True
    )
    spots_in = spread(spots.reshape(devices, slot_total)).reshape(devices, owned, capacity)
    rows_in = spread(rows_out.reshape(devices, slot_total, width))
    rows_in = rows_in.reshape(devices, owned, capacity, width)
    results = []
    for slot in range(owned):
        slot_rows = rows_in[:, slot].reshape(devices * capacity, width)
        slot_spots = spots_in[:, slot].reshape(devices * capacity)
        selector = (
            jnp.arange(front_size, dtype=jnp.int32)[:, None] == slot_spots[None, :]
        ).astype(jnp.bfloat16)
        assembled = jnp.dot(selector, slot_rows, preferred_element_type=jnp.float32)
        assembled = assembled.astype(jnp.bfloat16)
        results.append(jnp.dot(schur[slot], assembled, preferred_element_type=jnp.float32))
    return (adjoint, jnp.stack(results))


def solution(mesh):
    placed = (
        P("gx", "gy", None),
        P("gx", "gy", None),
        P("gx", "gy"),
        P(),
        P(("gx", "gy")),
        P(("gx", "gy"), None),
        P(("gx", "gy")),
        P(),
        P(("gx", "gy"), None, None),
    )
    return jax.shard_map(
        functools.partial(local, mesh.shape["gx"], mesh.shape["gy"]),
        mesh=mesh,
        in_specs=placed,
        out_specs=(P("gx", "gy", None), P(("gx", "gy"), None, None)),
        check_vma=False,
    )
```

```python
import functools

import jax
import jax.numpy as jnp
from jax import lax
from jax.experimental import pallas as pl
from jax.experimental.pallas import tpu as pltpu
from jax.sharding import PartitionSpec as P

LEVELS = 16

soft_floor = 0.001
relax_rate = 0.5

MESH = pl.DeviceIdType.MESH
PASSES = 3
SIDES = ((-1, 0), (1, 0), (0, -1), (0, 1), (-1, -1), (-1, 1), (1, -1), (1, 1))


def cell_weight(levels):
    ratio = levels.astype(jnp.float32) / LEVELS
    return soft_floor + (1.0 - soft_floor) * ratio * ratio * ratio


def relax_kernel(
    size_x,
    size_y,
    grad_ref,
    start_ref,
    weight_ref,
    blocks_ref,
    lam_ref,
    wide_ref,
    shifted_ref,
    line_ref,
    big_ref,
    edge_ref,
    edge_send_ref,
    row_in_ref,
    col_in_ref,
    send_sem,
    recv_sem,
):
    rows, cols, width = grad_ref.shape
    gx, gy = lax.axis_index("gx"), lax.axis_index("gy")

    def exists(side):
        dx, dy = side
        held = None
        for here, step, size in ((gx, dx, size_x), (gy, dy, size_y)):
            if step:
                inside = (here + step >= 0) & (here + step < size)
                held = inside if held is None else held & inside
        return held

    def place(side):
        return (gx + side[0], gy + side[1])

    row_in_ref[...] = jnp.zeros_like(row_in_ref)
    col_in_ref[...] = jnp.zeros_like(col_in_ref)

    barrier = pltpu.get_barrier_semaphore()
    for side in SIDES:

        @pl.when(exists(side))
        def _(side=side):
            pl.semaphore_signal(barrier, inc=1, device_id=place(side), device_id_type=MESH)

    for b in range(3):
        shifted_ref[b, 0] = jnp.zeros((cols, width), jnp.bfloat16)
        shifted_ref[b, rows + 1] = jnp.zeros((cols, width), jnp.bfloat16)
    line_ref[0:8, :] = jnp.zeros((8, width), jnp.float32)
    line_ref[8 + cols : 16 + cols, :] = jnp.zeros((8, width), jnp.float32)

    for i in range(4):
        for b in range(3):
            for j in range(2):
                a = j + 1 - i
                at = (pl.ds((3 * i + b) * width, width), pl.ds(j * width, width))
                if -1 <= a <= 1:
                    big_ref[at] = blocks_ref[3 * (a + 1) + b]
                else:
                    big_ref[at] = jnp.zeros((width, width), jnp.bfloat16)

    for r in range(rows):
        wide_ref[r] = jnp.broadcast_to(weight_ref[:, r : r + 1], (cols, width))

    def take_start(r, carry):
        lam_ref[r] = start_ref[r].astype(jnp.float32)
        return carry

    lax.fori_loop(0, rows, take_start, 0)

    near_x = 1 + jnp.minimum(gx, 1) + jnp.minimum(size_x - 1 - gx, 1)
    near_y = 1 + jnp.minimum(gy, 1) + jnp.minimum(size_y - 1 - gy, 1)
    pl.semaphore_wait(barrier, near_x * near_y - 1)

    def copies(step):
        made = []
        for n, side in enumerate(SIDES):
            if side[1] == 0:
                source = shifted_ref.at[1, 1 if side[0] < 0 else rows]
                target = row_in_ref.at[step, 1 if side[0] < 0 else 0]
            else:
                source = edge_send_ref.at[0 if side[1] < 0 else 1]
                target = col_in_ref.at[step, SIDES.index((-side[0], -side[1])) - 2]
            made.append(
                pltpu.make_async_remote_copy(
                    src_ref=source,
                    dst_ref=target,
                    send_sem=send_sem.at[step, n],
                    recv_sem=recv_sem.at[step, SIDES.index((-side[0], -side[1]))],
                    device_id=place(side),
                    device_id_type=MESH,
                )
            )
        return made

    def arrivals(step):
        made = []
        for n, side in enumerate(SIDES):
            if side[1] == 0:
                target = row_in_ref.at[step, 0 if side[0] < 0 else 1]
            else:
                target = col_in_ref.at[step, n - 2]
            made.append((side, target, recv_sem.at[step, n]))
        return made

    def spread():
        return [line_ref[9 - b : 9 - b + cols, :].astype(jnp.bfloat16) for b in range(3)]

    for step in range(PASSES):

        def produce(r, carry):
            scaled = wide_ref[r] * lam_ref[r]
            line_ref[8 : 8 + cols, :] = scaled
            left, middle, right = spread()
            shifted_ref[0, r + 1] = left
            shifted_ref[1, r + 1] = middle
            shifted_ref[2, r + 1] = right
            edge_ref[0, pl.ds(r, 1), :] = scaled[0:1, :]
            edge_ref[1, pl.ds(r, 1), :] = scaled[cols - 1 : cols, :]
            return carry

        lax.fori_loop(0, rows, produce, 0)
        edge_send_ref[...] = edge_ref[:, 0:rows, :].astype(jnp.bfloat16)

        sends = copies(step)
        for side, copy in zip(SIDES, sends):

            @pl.when(exists(side))
            def _(copy=copy):
                copy.start()

        def interior(t, carry):
            r = 4 * t
            lhs = jnp.concatenate(
                [
                    jnp.concatenate(
                        [shifted_ref[b, r + 2 * p + i] for i in range(4) for b in range(3)], axis=1
                    )
                    for p in range(2)
                ],
                axis=0,
            )
            image = jnp.dot(lhs, big_ref[...], preferred_element_type=jnp.float32)
            for p in range(2):
                for j in range(2):
                    at = r + 2 * p + j
                    part = image[p * cols : (p + 1) * cols, j * width : (j + 1) * width]
                    lam_ref[at] = lam_ref[at] + relax_rate * (
                        grad_ref[at].astype(jnp.float32) - part
                    )
            return carry

        lax.fori_loop(0, rows // 4, interior, 0)

        for n, (side, copy) in enumerate(zip(SIDES, sends)):

            @pl.when(exists(side))
            def _(copy=copy):
                copy.wait_send()

        for side, copy in zip(SIDES, sends):

            @pl.when(exists(side))
            def _(side=side, step=step):
                target, semaphore = [x[1:] for x in arrivals(step) if x[0] == side][0]
                pltpu.make_async_remote_copy(
                    src_ref=target,
                    dst_ref=target,
                    send_sem=send_sem.at[step, 0],
                    recv_sem=semaphore,
                    device_id=place(side),
                    device_id_type=MESH,
                ).wait_recv()

        for end in range(2):
            line_ref[8 : 8 + cols, :] = row_in_ref[step, end].astype(jnp.float32)
            lhs = jnp.concatenate(spread(), axis=1)
            depth = 3 * width
            piece = (
                big_ref[0:depth, 0:width]
                if end == 0
                else big_ref[3 * depth : 4 * depth, width : 2 * width]
            )
            more = jnp.dot(lhs, piece, preferred_element_type=jnp.float32)
            at = 0 if end == 0 else rows - 1
            lam_ref[at] = lam_ref[at] - relax_rate * more

        for end in range(2):
            edge_ref[end, 8 : 8 + rows, :] = col_in_ref[step, end].astype(jnp.float32)
            upper = col_in_ref[step, 2 + end].astype(jnp.float32)
            lower = col_in_ref[step, 4 + end].astype(jnp.float32)
            edge_ref[end, 7:8, :] = upper[rows - 1 : rows, :]
            edge_ref[end, 8 + rows : 9 + rows, :] = lower[0:1, :]
            b = 2 if end == 0 else 0
            more = jnp.zeros((rows, width), jnp.float32)
            for a in (-1, 0, 1):
                source = edge_ref[end, 8 - a : 8 - a + rows, :].astype(jnp.bfloat16)
                more = more + jnp.dot(
                    source, blocks_ref[3 * (a + 1) + b], preferred_element_type=jnp.float32
                )
            at = 0 if end == 0 else cols - 1
            for r in range(rows):
                lam_ref[r, at : at + 1, :] = (
                    lam_ref[r, at : at + 1, :] - relax_rate * more[r : r + 1, :]
                )


def relax(grad, start, weight, blocks, size_x, size_y):
    rows, cols, width = grad.shape
    vmem = pl.BlockSpec(memory_space=pltpu.VMEM)
    return pl.pallas_call(
        functools.partial(relax_kernel, size_x, size_y),
        out_shape=jax.ShapeDtypeStruct((rows, cols, width), jnp.float32),
        in_specs=[vmem] * 4,
        out_specs=vmem,
        scratch_shapes=[
            pltpu.VMEM((rows, cols, width), jnp.float32),
            pltpu.VMEM((3, rows + 2, cols, width), jnp.bfloat16),
            pltpu.VMEM((cols + 16, width), jnp.float32),
            pltpu.VMEM((12 * width, 2 * width), jnp.bfloat16),
            pltpu.VMEM((2, rows + 16, width), jnp.float32),
            pltpu.VMEM((2, rows, width), jnp.bfloat16),
            pltpu.VMEM((PASSES, 2, cols, width), jnp.bfloat16),
            pltpu.VMEM((PASSES, 6, rows, width), jnp.bfloat16),
            pltpu.SemaphoreType.DMA((PASSES, 8)),
            pltpu.SemaphoreType.DMA((PASSES, 8)),
        ],
        compiler_params=pltpu.CompilerParams(
            collective_id=0, has_side_effects=True, vmem_limit_bytes=48 * 1024 * 1024
        ),
        cost_estimate=pl.CostEstimate(
            flops=6 * 2 * rows * cols * width * 9 * width,
            bytes_accessed=8 * rows * cols * width,
            transcendentals=0,
        ),
    )(grad, start, weight, blocks)


def table_kernel(owned, front_ref, cell_ref, pos_ref, place_ref, cells_ref, spots_ref, sums_ref):
    count, capacity = cells_ref.shape
    total = front_ref.shape[1]
    block = 256
    order = lax.broadcasted_iota(jnp.int32, (count, count), 0)
    moved = (order == place_ref[...]).astype(jnp.float32).astype(jnp.bfloat16)
    before = (
        lax.broadcasted_iota(jnp.int32, (block, block), 0)
        < lax.broadcasted_iota(jnp.int32, (block, block), 1)
    )
    before = before.astype(jnp.float32).astype(jnp.bfloat16)
    carry = jnp.zeros((count, 1), jnp.float32)
    sums_ref[...] = jnp.zeros_like(sums_ref)
    for n in range(total // block):
        at = slice(n * block, (n + 1) * block)
        named = lax.broadcasted_iota(jnp.int32, (count, block), 0) == front_ref[:, at]
        named = named.astype(jnp.float32).astype(jnp.bfloat16)
        member = jnp.dot(moved, named, preferred_element_type=jnp.float32)
        inside = jnp.dot(
            member.astype(jnp.bfloat16), before, preferred_element_type=jnp.float32
        )
        rank = jnp.sum(member * (inside + carry), axis=0, keepdims=True)
        carry = carry + jnp.sum(member, axis=1, keepdims=True)
        slot = lax.broadcasted_iota(jnp.int32, (capacity, block), 0) == rank.astype(jnp.int32)
        slot = slot.astype(jnp.float32).astype(jnp.bfloat16)
        cell, pos = cell_ref[:, at], pos_ref[:, at]
        pieces = (cell // 64, cell % 64, pos // 16, pos % 16 + 1)
        lhs = jnp.concatenate([member * p.astype(jnp.float32) for p in pieces], axis=0)
        sums_ref[...] += lax.dot_general(
            lhs.astype(jnp.bfloat16),
            slot,
            (((1,), (1,)), ((), ())),
            preferred_element_type=jnp.float32,
        )
    part = [sums_ref[n * count : (n + 1) * count, :].astype(jnp.int32) for n in range(4)]
    cells_ref[...] = part[0] * 64 + part[1]
    spots = part[2] * 16 + part[3] - 1
    size_y = spots_ref.shape[0]
    size_x = count // (size_y * owned)
    for x in range(size_x):
        for y in range(size_y):
            at = (x * size_y + y) * owned
            spots_ref[y, x * owned : (x + 1) * owned, :] = spots[at : at + owned, :]


def row_table(row_front, row_cells, row_pos, front_place, capacity, owned, size_y):
    count = front_place.shape[0]
    return pl.pallas_call(
        functools.partial(table_kernel, owned),
        out_shape=(
            jax.ShapeDtypeStruct((count, capacity), jnp.int32),
            jax.ShapeDtypeStruct((size_y, count // size_y, capacity), jnp.int32),
        ),
        in_specs=[pl.BlockSpec(memory_space=pltpu.VMEM)] * 4,
        out_specs=(pl.BlockSpec(memory_space=pltpu.VMEM),) * 2,
        scratch_shapes=[pltpu.VMEM((4 * count, capacity), jnp.float32)],
        compiler_params=pltpu.CompilerParams(vmem_limit_bytes=32 * 1024 * 1024),
    )(
        row_front.reshape(1, -1),
        row_cells.reshape(1, -1),
        row_pos.reshape(1, -1),
        front_place.reshape(1, -1),
    )


def route_kernel(
    size_x,
    size_y,
    cells_ref,
    spots_ref,
    field_ref,
    schur_ref,
    out_ref,
    held_ref,
    rows_send_ref,
    rows_in_ref,
    spots_in_ref,
    dense_send_ref,
    dense_in_ref,
    own_ref,
    rows_send_sem,
    rows_in_sem,
    spots_send_sem,
    spots_in_sem,
    dense_send_sem,
    dense_in_sem,
):
    owned, size, width = out_ref.shape
    capacity = cells_ref.shape[1]
    gx, gy = lax.axis_index("gx"), lax.axis_index("gy")
    barrier = pltpu.get_barrier_semaphore()
    for u in range(1, size_y):
        pl.semaphore_signal(
            barrier, inc=1, device_id=(gx, lax.rem(gy + u, size_y)), device_id_type=MESH
        )
    for s in range(1, size_x):
        pl.semaphore_signal(
            barrier, inc=1, device_id=(lax.rem(gx + s, size_x), gy), device_id_type=MESH
        )
    pl.semaphore_wait(barrier, size_x + size_y - 2)

    order = sorted(range(size_x), key=lambda s: (s == 0, abs(2 * s - size_x)))

    def to_peer(source, target, send_sem, recv_sem, device):
        return pltpu.make_async_remote_copy(
            src_ref=source,
            dst_ref=target,
            send_sem=send_sem,
            recv_sem=recv_sem,
            device_id=device,
            device_id_type=MESH,
        )

    def spots_copy(u):
        peer = lax.rem(gy + u, size_y)
        return to_peer(
            spots_ref.at[peer],
            spots_in_ref.at[u],
            spots_send_sem.at[u],
            spots_in_sem.at[u],
            (gx, peer),
        )

    def rows_copy(t, u):
        peer = lax.rem(gy + u, size_y)
        return to_peer(
            rows_send_ref.at[t, peer],
            rows_in_ref.at[t, u],
            rows_send_sem.at[t, u],
            rows_in_sem.at[t, u],
            (gx, peer),
        )

    def dense_copy(t):
        s = order[t]
        return to_peer(
            dense_send_ref.at[t],
            dense_in_ref.at[t],
            dense_send_sem.at[t],
            dense_in_sem.at[t],
            (lax.rem(gx + s, size_x), gy),
        )

    for u in range(1, size_y):
        spots_copy(u).start()

    def gather(t):
        first = lax.rem(gx + order[t], size_x) * (size_y * owned)

        def one_front(q, carry):
            base = pl.multiple_of(q * capacity, capacity)
            for r in range(capacity):
                cell = cells_ref[first + q, r]
                held_ref[pl.ds(base + r, 1), :] = field_ref[pl.ds(cell, 1), :]
            return carry

        lax.fori_loop(0, size_y * owned, one_front, 0)
        depth = owned * capacity
        for y in range(size_y):
            rows_send_ref[t, y] = held_ref[y * depth : (y + 1) * depth, :].astype(jnp.bfloat16)
        for u in range(1, size_y):
            rows_copy(t, u).start()

    def assemble(t):
        plane = lax.rem(gx + order[t], size_x)
        if t == 0:
            for u in range(1, size_y):
                spots_copy(u).wait_recv()
        for u in range(1, size_y):
            rows_copy(t, u).wait_recv()
        positions = lax.broadcasted_iota(jnp.int32, (size, capacity), 0)
        for o in range(owned):
            line = pl.ds(plane * owned + o, 1)
            part = pl.ds(o * capacity, capacity)
            selectors, sources = [], []
            for u in range(size_y):
                spot = spots_ref[gy, line, :] if u == 0 else spots_in_ref[u, line, :]
                selectors.append(jnp.where(positions == spot, 1.0, 0.0).astype(jnp.bfloat16))
                sources.append(rows_send_ref[t, gy, part, :] if u == 0 else rows_in_ref[t, u, part, :])
            if capacity % 128 == 0:
                selectors = [jnp.concatenate(selectors, axis=1)]
                sources = [jnp.concatenate(sources, axis=0)]
            total = jnp.zeros((size, width), jnp.float32)
            for selector, source in zip(selectors, sources):
                total = total + jnp.dot(selector, source, preferred_element_type=jnp.float32)
            if order[t]:
                dense_send_ref[t, o] = total.astype(jnp.bfloat16)
            else:
                own_ref[o] = total
        if order[t]:
            dense_copy(t).start()

    gather(0)
    for t in range(1, size_x):
        gather(t)
        assemble(t - 1)
    assemble(size_x - 1)

    for t in range(size_x - 1):
        dense_copy(t).wait_recv()
    for o in range(owned):
        total = own_ref[o]
        for t in range(size_x - 1):
            total = total + dense_in_ref[t, o].astype(jnp.float32)
        out_ref[o] = jnp.dot(
            schur_ref[o], total.astype(jnp.bfloat16), preferred_element_type=jnp.float32
        )

    for u in range(1, size_y):
        spots_copy(u).wait_send()
        for t in range(size_x):
            rows_copy(t, u).wait_send()
    for t in range(size_x - 1):
        dense_copy(t).wait_send()


def route(cells, spots, field, schur, size_x, size_y):
    owned, size, _ = schur.shape
    capacity, width = cells.shape[1], field.shape[1]
    vmem = pl.BlockSpec(memory_space=pltpu.VMEM)
    dma = pltpu.SemaphoreType.DMA
    return pl.pallas_call(
        functools.partial(route_kernel, size_x, size_y),
        out_shape=jax.ShapeDtypeStruct((owned, size, width), jnp.float32),
        in_specs=[pl.BlockSpec(memory_space=pltpu.SMEM), vmem, vmem, vmem],
        out_specs=vmem,
        scratch_shapes=[
            pltpu.VMEM((size_y * owned * capacity, width), jnp.float32),
            pltpu.VMEM((size_x, size_y, owned * capacity, width), jnp.bfloat16),
            pltpu.VMEM((size_x, size_y, owned * capacity, width), jnp.bfloat16),
            pltpu.VMEM(spots.shape, jnp.int32),
            pltpu.VMEM((size_x - 1, owned, size, width), jnp.bfloat16),
            pltpu.VMEM((size_x - 1, owned, size, width), jnp.bfloat16),
            pltpu.VMEM((owned, size, width), jnp.float32),
            dma((size_x, size_y)),
            dma((size_x, size_y)),
            dma((size_y,)),
            dma((size_y,)),
            dma((size_x - 1,)),
            dma((size_x - 1,)),
        ],
        compiler_params=pltpu.CompilerParams(
            collective_id=1, has_side_effects=True, vmem_limit_bytes=48 * 1024 * 1024
        ),
    )(cells, spots, field, schur)


def local(
    size_x,
    size_y,
    objective_grad,
    adjoint_start,
    levels,
    stiffness,
    row_cells,
    row_front,
    row_pos,
    front_place,
    schur,
):
    rows, cols, width = objective_grad.shape
    freedom = stiffness.shape[1]
    cases = width // freedom
    same = jnp.eye(cases, dtype=stiffness.dtype)
    blocks = (same[None, :, None, :, None] * stiffness[:, None, :, None, :]).reshape(
        9, width, width
    )
    capacity = 2 * row_cells.shape[0] // front_place.shape[0]
    cells, spots = row_table(
        row_front, row_cells, row_pos, front_place, capacity, schur.shape[0], size_y
    )
    adjoint = relax(
        objective_grad, adjoint_start, cell_weight(levels).T, blocks, size_x, size_y
    )
    field = adjoint.reshape(rows * cols, width)
    return (adjoint, route(cells, spots, field, schur, size_x, size_y))


def solution(mesh):
    placed = (
        P("gx", "gy", None),
        P("gx", "gy", None),
        P("gx", "gy"),
        P(),
        P(("gx", "gy")),
        P(("gx", "gy"), None),
        P(("gx", "gy")),
        P(),
        P(("gx", "gy"), None, None),
    )
    return jax.shard_map(
        functools.partial(local, mesh.shape["gx"], mesh.shape["gy"]),
        mesh=mesh,
        in_specs=placed,
        out_specs=(P("gx", "gy", None), P(("gx", "gy"), None, None)),
        check_vma=False,
    )
```

```python
import functools

import jax
import jax.numpy as jnp
from jax import lax
from jax.experimental import pallas as pl
from jax.experimental.pallas import tpu as pltpu
from jax.sharding import PartitionSpec as P

LEVELS = 16

soft_floor = 0.001
relax_rate = 0.5

MESH = pl.DeviceIdType.MESH
PASSES = 3
SIDES = ((-1, 0), (1, 0), (0, -1), (0, 1), (-1, -1), (-1, 1), (1, -1), (1, 1))


def cell_weight(levels):
    ratio = levels.astype(jnp.float32) / LEVELS
    return soft_floor + (1.0 - soft_floor) * ratio * ratio * ratio


def relax_part(
    size_x,
    size_y,
    grad_ref,
    levels_ref,
    stiffness_ref,
    blocks_ref,
    lam_ref,
    start_ref,
    wide_ref,
    shifted_ref,
    line_ref,
    big_ref,
    edge_ref,
    edge_send_ref,
    row_in_ref,
    col_in_ref,
    send_sem,
    recv_sem,
    incoming,
):
    rows, cols, width = grad_ref.shape
    gx, gy = lax.axis_index("gx"), lax.axis_index("gy")

    def exists(side):
        dx, dy = side
        held = None
        for here, step, size in ((gx, dx, size_x), (gy, dy, size_y)):
            if step:
                inside = (here + step >= 0) & (here + step < size)
                held = inside if held is None else held & inside
        return held

    def place(side):
        return (gx + side[0], gy + side[1])

    row_in_ref[...] = jnp.zeros_like(row_in_ref)
    col_in_ref[...] = jnp.zeros_like(col_in_ref)

    barrier = pltpu.get_barrier_semaphore()
    for side in SIDES[4:]:

        @pl.when(exists(side))
        def _(side=side):
            pl.semaphore_signal(barrier, inc=1, device_id=place(side), device_id_type=MESH)

    for u in range(1, size_y):
        pl.semaphore_signal(
            barrier, inc=1, device_id=(gx, lax.rem(gy + u, size_y)), device_id_type=MESH
        )
    for u in range(1, size_x):
        pl.semaphore_signal(
            barrier, inc=1, device_id=(lax.rem(gx + u, size_x), gy), device_id_type=MESH
        )

    for b in range(3):
        shifted_ref[b, 0] = jnp.zeros((cols, width), jnp.bfloat16)
        shifted_ref[b, rows + 1] = jnp.zeros((cols, width), jnp.bfloat16)
    line_ref[0:8, :] = jnp.zeros((8, width), jnp.float32)
    line_ref[8 + cols : 16 + cols, :] = jnp.zeros((8, width), jnp.float32)

    incoming("stiffness")
    freedom = stiffness_ref.shape[1]
    blocks_ref[...] = jnp.zeros_like(blocks_ref)
    for n in range(9):
        block = stiffness_ref[n]
        empty = jnp.zeros((freedom, freedom), jnp.bfloat16)
        for c in range(width // freedom):
            parts = [block if e == c else empty for e in range(width // freedom)]
            blocks_ref[n, c * freedom : (c + 1) * freedom, :] = jnp.concatenate(parts, axis=1)

    for i in range(4):
        for b in range(3):
            for j in range(2):
                a = j + 1 - i
                at = (pl.ds((3 * i + b) * width, width), pl.ds(j * width, width))
                if -1 <= a <= 1:
                    big_ref[at] = blocks_ref[3 * (a + 1) + b]
                else:
                    big_ref[at] = jnp.zeros((width, width), jnp.bfloat16)

    incoming("levels")
    weight = cell_weight(levels_ref[...]).T
    for r in range(rows):
        wide_ref[r] = jnp.broadcast_to(weight[:, r : r + 1], (cols, width))

    def line_of(r):
        return pl.ds(pl.multiple_of(r * cols, cols), cols)

    incoming("start")

    def take_start(r, carry):
        lam_ref[line_of(r), :] = start_ref[r].astype(jnp.float32)
        return carry

    lax.fori_loop(0, rows, take_start, 0)

    near_x = jnp.minimum(gx, 1) + jnp.minimum(size_x - 1 - gx, 1)
    near_y = jnp.minimum(gy, 1) + jnp.minimum(size_y - 1 - gy, 1)
    pl.semaphore_wait(barrier, near_x * near_y + size_x + size_y - 2)

    def copies(step):
        made = []
        for n, side in enumerate(SIDES):
            if side[1] == 0:
                source = shifted_ref.at[1, 1 if side[0] < 0 else rows]
                target = row_in_ref.at[step, 1 if side[0] < 0 else 0]
            else:
                source = edge_send_ref.at[0 if side[1] < 0 else 1]
                target = col_in_ref.at[step, SIDES.index((-side[0], -side[1])) - 2]
            made.append(
                pltpu.make_async_remote_copy(
                    src_ref=source,
                    dst_ref=target,
                    send_sem=send_sem.at[step, n],
                    recv_sem=recv_sem.at[step, SIDES.index((-side[0], -side[1]))],
                    device_id=place(side),
                    device_id_type=MESH,
                )
            )
        return made

    def arrivals(step):
        made = []
        for n, side in enumerate(SIDES):
            if side[1] == 0:
                target = row_in_ref.at[step, 0 if side[0] < 0 else 1]
            else:
                target = col_in_ref.at[step, n - 2]
            made.append((side, target, recv_sem.at[step, n]))
        return made

    def spread():
        return [line_ref[9 - b : 9 - b + cols, :].astype(jnp.bfloat16) for b in range(3)]

    for step in range(PASSES):

        def produce(r, carry):
            scaled = wide_ref[r] * lam_ref[line_of(r), :]
            line_ref[8 : 8 + cols, :] = scaled
            left, middle, right = spread()
            shifted_ref[0, r + 1] = left
            shifted_ref[1, r + 1] = middle
            shifted_ref[2, r + 1] = right
            edge_ref[0, pl.ds(r, 1), :] = scaled[0:1, :]
            edge_ref[1, pl.ds(r, 1), :] = scaled[cols - 1 : cols, :]
            return carry

        lax.fori_loop(0, rows, produce, 0)
        edge_send_ref[...] = edge_ref[:, 0:rows, :].astype(jnp.bfloat16)

        sends = copies(step)
        for side, copy in zip(SIDES, sends):

            @pl.when(exists(side))
            def _(copy=copy):
                copy.start()

        if step == 0:
            incoming("grad")

        def interior(t, carry):
            r = 4 * t
            lhs = jnp.concatenate(
                [
                    jnp.concatenate(
                        [shifted_ref[b, r + 2 * p + i] for i in range(4) for b in range(3)], axis=1
                    )
                    for p in range(2)
                ],
                axis=0,
            )
            image = jnp.dot(lhs, big_ref[...], preferred_element_type=jnp.float32)
            for p in range(2):
                for j in range(2):
                    at = r + 2 * p + j
                    part = image[p * cols : (p + 1) * cols, j * width : (j + 1) * width]
                    line = line_of(at)
                    lam_ref[line, :] = lam_ref[line, :] + relax_rate * (
                        grad_ref[at].astype(jnp.float32) - part
                    )
            return carry

        lax.fori_loop(0, rows // 4, interior, 0)

        for n, (side, copy) in enumerate(zip(SIDES, sends)):

            @pl.when(exists(side))
            def _(copy=copy):
                copy.wait_send()

        for side, copy in zip(SIDES, sends):

            @pl.when(exists(side))
            def _(side=side, step=step):
                target, semaphore = [x[1:] for x in arrivals(step) if x[0] == side][0]
                pltpu.make_async_remote_copy(
                    src_ref=target,
                    dst_ref=target,
                    send_sem=send_sem.at[step, 0],
                    recv_sem=semaphore,
                    device_id=place(side),
                    device_id_type=MESH,
                ).wait_recv()

        for end in range(2):
            line_ref[8 : 8 + cols, :] = row_in_ref[step, end].astype(jnp.float32)
            lhs = jnp.concatenate(spread(), axis=1)
            depth = 3 * width
            piece = (
                big_ref[0:depth, 0:width]
                if end == 0
                else big_ref[3 * depth : 4 * depth, width : 2 * width]
            )
            more = jnp.dot(lhs, piece, preferred_element_type=jnp.float32)
            line = line_of(0 if end == 0 else rows - 1)
            lam_ref[line, :] = lam_ref[line, :] - relax_rate * more

        for end in range(2):
            edge_ref[end, 8 : 8 + rows, :] = col_in_ref[step, end].astype(jnp.float32)
            upper = col_in_ref[step, 2 + end].astype(jnp.float32)
            lower = col_in_ref[step, 4 + end].astype(jnp.float32)
            edge_ref[end, 7:8, :] = upper[rows - 1 : rows, :]
            edge_ref[end, 8 + rows : 9 + rows, :] = lower[0:1, :]
            b = 2 if end == 0 else 0
            more = jnp.zeros((rows, width), jnp.float32)
            for a in (-1, 0, 1):
                source = edge_ref[end, 8 - a : 8 - a + rows, :].astype(jnp.bfloat16)
                more = more + jnp.dot(
                    source, blocks_ref[3 * (a + 1) + b], preferred_element_type=jnp.float32
                )
            at = 0 if end == 0 else cols - 1
            for r in range(rows):
                cell = slice(r * cols + at, r * cols + at + 1)
                lam_ref[cell, :] = lam_ref[cell, :] - relax_rate * more[r : r + 1, :]


def table_part(owned, front_ref, cell_ref, pos_ref, place_ref, cells_ref, spots_ref, sums_ref):
    count, capacity = cells_ref.shape
    total = front_ref.shape[1]
    block = 256
    order = lax.broadcasted_iota(jnp.int32, (count, count), 0)
    moved = (order == place_ref[...]).astype(jnp.float32).astype(jnp.bfloat16)
    before = (
        lax.broadcasted_iota(jnp.int32, (block, block), 0)
        < lax.broadcasted_iota(jnp.int32, (block, block), 1)
    )
    before = before.astype(jnp.float32).astype(jnp.bfloat16)
    carry = jnp.zeros((count, 1), jnp.float32)
    sums_ref[...] = jnp.zeros_like(sums_ref)
    for n in range(total // block):
        at = slice(n * block, (n + 1) * block)
        named = lax.broadcasted_iota(jnp.int32, (count, block), 0) == front_ref[:, at]
        named = named.astype(jnp.float32).astype(jnp.bfloat16)
        member = jnp.dot(moved, named, preferred_element_type=jnp.float32)
        inside = jnp.dot(
            member.astype(jnp.bfloat16), before, preferred_element_type=jnp.float32
        )
        rank = jnp.sum(member * (inside + carry), axis=0, keepdims=True)
        carry = carry + jnp.sum(member, axis=1, keepdims=True)
        slot = lax.broadcasted_iota(jnp.int32, (capacity, block), 0) == rank.astype(jnp.int32)
        slot = slot.astype(jnp.float32).astype(jnp.bfloat16)
        cell, pos = cell_ref[:, at], pos_ref[:, at]
        pieces = (cell // 64, cell % 64, pos // 16, pos % 16 + 1)
        lhs = jnp.concatenate([member * p.astype(jnp.float32) for p in pieces], axis=0)
        sums_ref[...] += lax.dot_general(
            lhs.astype(jnp.bfloat16),
            slot,
            (((1,), (1,)), ((), ())),
            preferred_element_type=jnp.float32,
        )
    part = [sums_ref[n * count : (n + 1) * count, :].astype(jnp.int32) for n in range(4)]
    cells_ref[...] = part[0] * 64 + part[1]
    spots = part[2] * 16 + part[3] - 1
    size_y = spots_ref.shape[0]
    size_x = count // (size_y * owned)
    for x in range(size_x):
        for y in range(size_y):
            at = (x * size_y + y) * owned
            spots_ref[y, x * owned : (x + 1) * owned, :] = spots[at : at + owned, :]


def route_part(
    size_x,
    size_y,
    cells_ref,
    spots_ref,
    field_ref,
    schur_ref,
    out_ref,
    held_ref,
    rows_send_ref,
    rows_in_ref,
    spots_in_ref,
    dense_send_ref,
    dense_in_ref,
    own_ref,
    rows_send_sem,
    rows_in_sem,
    spots_send_sem,
    spots_in_sem,
    dense_send_sem,
    dense_in_sem,
):
    owned, size, width = out_ref.shape
    capacity = cells_ref.shape[1]
    gx, gy = lax.axis_index("gx"), lax.axis_index("gy")
    order = sorted(range(size_x), key=lambda s: (s == 0, abs(2 * s - size_x)))

    def to_peer(source, target, send_sem, recv_sem, device):
        return pltpu.make_async_remote_copy(
            src_ref=source,
            dst_ref=target,
            send_sem=send_sem,
            recv_sem=recv_sem,
            device_id=device,
            device_id_type=MESH,
        )

    def spots_copy(u):
        peer = lax.rem(gy + u, size_y)
        return to_peer(
            spots_ref.at[peer],
            spots_in_ref.at[u],
            spots_send_sem.at[u],
            spots_in_sem.at[u],
            (gx, peer),
        )

    def rows_copy(t, u):
        peer = lax.rem(gy + u, size_y)
        return to_peer(
            rows_send_ref.at[t, peer],
            rows_in_ref.at[t, u],
            rows_send_sem.at[t, u],
            rows_in_sem.at[t, u],
            (gx, peer),
        )

    def dense_copy(t):
        s = order[t]
        return to_peer(
            dense_send_ref.at[t],
            dense_in_ref.at[t],
            dense_send_sem.at[t],
            dense_in_sem.at[t],
            (lax.rem(gx + s, size_x), gy),
        )

    for u in range(1, size_y):
        spots_copy(u).start()

    def gather(t):
        first = lax.rem(gx + order[t], size_x) * (size_y * owned)

        def one_front(q, carry):
            base = pl.multiple_of(q * capacity, capacity)
            for r in range(capacity):
                cell = cells_ref[first + q, r]
                held_ref[pl.ds(base + r, 1), :] = field_ref[pl.ds(cell, 1), :]
            return carry

        lax.fori_loop(0, size_y * owned, one_front, 0)
        depth = owned * capacity
        for y in range(size_y):
            rows_send_ref[t, y] = held_ref[y * depth : (y + 1) * depth, :].astype(jnp.bfloat16)
        for u in range(1, size_y):
            rows_copy(t, u).start()

    def assemble(t):
        plane = lax.rem(gx + order[t], size_x)
        if t == 0:
            for u in range(1, size_y):
                spots_copy(u).wait_recv()
        for u in range(1, size_y):
            rows_copy(t, u).wait_recv()
        positions = lax.broadcasted_iota(jnp.int32, (size, capacity), 0)
        for o in range(owned):
            line = pl.ds(plane * owned + o, 1)
            part = pl.ds(o * capacity, capacity)
            selectors, sources = [], []
            for u in range(size_y):
                spot = spots_ref[gy, line, :] if u == 0 else spots_in_ref[u, line, :]
                selectors.append(jnp.where(positions == spot, 1.0, 0.0).astype(jnp.bfloat16))
                sources.append(rows_send_ref[t, gy, part, :] if u == 0 else rows_in_ref[t, u, part, :])
            if capacity % 128 == 0:
                selectors = [jnp.concatenate(selectors, axis=1)]
                sources = [jnp.concatenate(sources, axis=0)]
            total = jnp.zeros((size, width), jnp.float32)
            for selector, source in zip(selectors, sources):
                total = total + jnp.dot(selector, source, preferred_element_type=jnp.float32)
            if order[t]:
                dense_send_ref[t, o] = total.astype(jnp.bfloat16)
            else:
                own_ref[o] = total
        if order[t]:
            dense_copy(t).start()

    gather(0)
    for t in range(1, size_x):
        gather(t)
        assemble(t - 1)
    assemble(size_x - 1)

    for t in range(size_x - 1):
        dense_copy(t).wait_recv()
    for o in range(owned):
        total = own_ref[o]
        for t in range(size_x - 1):
            total = total + dense_in_ref[t, o].astype(jnp.float32)
        out_ref[o] = jnp.dot(
            schur_ref[o], total.astype(jnp.bfloat16), preferred_element_type=jnp.float32
        )

    for u in range(1, size_y):
        spots_copy(u).wait_send()
        for t in range(size_x):
            rows_copy(t, u).wait_send()
    for t in range(size_x - 1):
        dense_copy(t).wait_send()


NAMES = ("grad", "start", "levels", "stiffness", "schur")


def table_kernel(owned, *refs):
    given, (cells_ref, spots_ref), held = refs[:4], refs[4:6], refs[6:10]
    sums_ref, in_sem = refs[10:]
    copies = [
        pltpu.make_async_copy(source, target, in_sem.at[n])
        for n, (source, target) in enumerate(zip(given, held))
    ]
    for copy in copies:
        copy.start()
    for copy in copies:
        copy.wait()
    table_part(owned, *held, cells_ref, spots_ref, sums_ref)


def row_table(given, capacity, owned, size_y):
    count = given[3].shape[1]
    return pl.pallas_call(
        functools.partial(table_kernel, owned),
        out_shape=(
            jax.ShapeDtypeStruct((count, capacity), jnp.int32),
            jax.ShapeDtypeStruct((size_y, count // size_y, capacity), jnp.int32),
        ),
        in_specs=[pl.BlockSpec(memory_space=pl.ANY)] * 4,
        out_specs=(pl.BlockSpec(memory_space=pltpu.VMEM),) * 2,
        scratch_shapes=[
            *[pltpu.VMEM(x.shape, x.dtype) for x in given],
            pltpu.VMEM((4 * count, capacity), jnp.float32),
            pltpu.SemaphoreType.DMA((4,)),
        ],
        compiler_params=pltpu.CompilerParams(vmem_limit_bytes=60 * 1024 * 1024),
    )(*given)


def whole_kernel(size_x, size_y, *refs):
    count = len(NAMES)
    given = dict(zip(NAMES, refs[:count]))
    cells_ref, spots_ref, lam_ref, out_ref = refs[count : count + 4]
    held = dict(zip(NAMES, refs[count + 4 : 2 * count + 4]))
    in_sem, blocks_ref = refs[2 * count + 4 : 2 * count + 6]
    relax_refs = refs[2 * count + 6 : 2 * count + 16]
    route_refs = refs[2 * count + 16 :]

    def copy_in(name):
        return pltpu.make_async_copy(given[name], held[name], in_sem.at[NAMES.index(name)])

    for name in ("stiffness", "levels", "start", "grad", "schur"):
        copy_in(name).start()

    def incoming(name):
        copy_in(name).wait()

    relax_part(
        size_x,
        size_y,
        held["grad"],
        held["levels"],
        held["stiffness"],
        blocks_ref,
        lam_ref,
        held["start"],
        *relax_refs,
        incoming,
    )
    incoming("schur")
    route_part(
        size_x,
        size_y,
        cells_ref,
        spots_ref,
        lam_ref,
        held["schur"],
        out_ref,
        *route_refs,
    )


def local(
    size_x,
    size_y,
    objective_grad,
    adjoint_start,
    levels,
    stiffness,
    row_cells,
    row_front,
    row_pos,
    front_place,
    schur,
):
    rows, cols, width = objective_grad.shape
    owned, size, _ = schur.shape
    count = front_place.shape[0]
    capacity = 2 * row_cells.shape[0] // count
    listed = [x.reshape(1, -1) for x in (row_front, row_cells, row_pos, front_place)]
    cells, spots = row_table(listed, capacity, owned, size_y)
    given = (objective_grad, adjoint_start, levels, stiffness, schur)
    vmem = pl.BlockSpec(memory_space=pltpu.VMEM)
    dma = pltpu.SemaphoreType.DMA
    adjoint, values = pl.pallas_call(
        functools.partial(whole_kernel, size_x, size_y),
        out_shape=(
            jax.ShapeDtypeStruct((rows * cols, width), jnp.float32),
            jax.ShapeDtypeStruct((owned, size, width), jnp.float32),
        ),
        in_specs=[pl.BlockSpec(memory_space=pl.ANY)] * len(given)
        + [pl.BlockSpec(memory_space=pltpu.SMEM), vmem],
        out_specs=(vmem, vmem),
        scratch_shapes=[
            *[pltpu.VMEM(x.shape, x.dtype) for x in given],
            dma((len(given),)),
            pltpu.VMEM((9, width, width), jnp.bfloat16),
            pltpu.VMEM((rows, cols, width), jnp.float32),
            pltpu.VMEM((3, rows + 2, cols, width), jnp.bfloat16),
            pltpu.VMEM((cols + 16, width), jnp.float32),
            pltpu.VMEM((12 * width, 2 * width), jnp.bfloat16),
            pltpu.VMEM((2, rows + 16, width), jnp.float32),
            pltpu.VMEM((2, rows, width), jnp.bfloat16),
            pltpu.VMEM((PASSES, 2, cols, width), jnp.bfloat16),
            pltpu.VMEM((PASSES, 6, rows, width), jnp.bfloat16),
            dma((PASSES, 8)),
            dma((PASSES, 8)),
            pltpu.VMEM((size_y * owned * capacity, width), jnp.float32),
            pltpu.VMEM((size_x, size_y, owned * capacity, width), jnp.bfloat16),
            pltpu.VMEM((size_x, size_y, owned * capacity, width), jnp.bfloat16),
            pltpu.VMEM(spots.shape, jnp.int32),
            pltpu.VMEM((size_x - 1, owned, size, width), jnp.bfloat16),
            pltpu.VMEM((size_x - 1, owned, size, width), jnp.bfloat16),
            pltpu.VMEM((owned, size, width), jnp.float32),
            dma((size_x, size_y)),
            dma((size_x, size_y)),
            dma((size_y,)),
            dma((size_y,)),
            dma((size_x - 1,)),
            dma((size_x - 1,)),
        ],
        compiler_params=pltpu.CompilerParams(
            collective_id=0, has_side_effects=True, vmem_limit_bytes=56 * 1024 * 1024
        ),
    )(*given, cells, spots)
    return (adjoint.reshape(rows, cols, width), values)


def solution(mesh):
    placed = (
        P("gx", "gy", None),
        P("gx", "gy", None),
        P("gx", "gy"),
        P(),
        P(("gx", "gy")),
        P(("gx", "gy"), None),
        P(("gx", "gy")),
        P(),
        P(("gx", "gy"), None, None),
    )
    return jax.shard_map(
        functools.partial(local, mesh.shape["gx"], mesh.shape["gy"]),
        mesh=mesh,
        in_specs=placed,
        out_specs=(P("gx", "gy", None), P(("gx", "gy"), None, None)),
        check_vma=False,
    )
```
